1024 devices in a mesh: fsdp: 128 (over z, x), tensor: 8 (over y, core).
Axes of the slice: x: 4, y: 4, z: 32, core: 2. Of those that a mesh axis runs over, the one named last changes fastest.
Arguments:
- momentum: bfloat16 [16384, 26624], P('fsdp', 'tensor'), may hold values from -6 to 6
- gradient: bfloat16 [16384, 26624], P('fsdp', 'tensor')
- basis: float32 [26624, 128], P(('tensor', 'fsdp')), may hold values from -0.0390625 to 0.0390625
Outputs:
- update: bfloat16 [16384, 26624], P('fsdp', 'tensor')
- new_momentum: bfloat16 [16384, 26624], P('fsdp', 'tensor')
The draws below stay inside these ranges and needn't reach their ends.
All inputs are finite; a program needn't handle non-finite values.
Results may differ from the reference program's by a relative error of at most 0.007.
The reference program's roundings to bfloat16 on the way count: a program that leaves them out, or rounds other values in their place, can miss the bound.
Values may be sent and summed in bfloat16 or wider, within the bound.
A program may use at most 32 MiB of HBM per device.

```python
import math
import jax
import jax.numpy as jnp
from jax import lax

D = 16384
FF = 26624
RANK = 128


def draw_gradient(key, part):
    key = jax.random.fold_in(key, 11)
    first, second, third = jax.random.split(key, 3)
    position = jnp.arange(FF, dtype=jnp.float32) / max(FF - 1, 1)
    col_scale = jnp.power(3.0, position) * jnp.exp(jax.random.uniform(second, (FF,), jnp.float32, 0.0, math.log(3.0)))
    row_scale = jnp.exp(jax.random.uniform(third, (D, 1), jnp.float32, 0.0, math.log(10.0)))
    base = jax.random.normal(first, (D, FF), jnp.float32)
    return (0.3 * base * row_scale * col_scale).astype(jnp.bfloat16)


def steps_of(key, dims, cuts, low, top_value):
    level, own = 1.0, jax.random.fold_in(key, 6)
    for dim, shards_of in cuts:
        draws = jnp.exp(jax.random.uniform(jax.random.fold_in(own, dim), (shards_of,), jnp.float32, low / len(cuts), top_value / len(cuts)))
        level = level * jnp.repeat(draws, dims[dim] // shards_of).reshape([-1 if axis == dim else 1 for axis in range(len(dims))])
    return level


def scatter_about(rng, dims, scale, bound, cuts=(), held_as=jnp.bfloat16):
    gain = steps_of(rng, dims, cuts, -0.22, 0.18) if cuts else 1.0
    result = jax.random.normal(rng, dims, jnp.float32) * scale * gain
    return jnp.minimum(jnp.maximum(result, -bound), bound).astype(held_as)


def setup_inputs(seed: int = 0) -> dict:
    arg_keys = jax.random.split(jax.random.key(seed), 4)
    momentum = scatter_about(arg_keys[0], (D, FF), 1.0, 6.0, ((0, 128), (1, 8)))
    gradient = draw_gradient(jax.random.fold_in(arg_keys[3], 71), 0)
    basis = scatter_about(arg_keys[2], (FF, RANK), FF ** -0.5, 0.0390625, ((0, 1024),), jnp.float32)
    return dict(momentum=momentum, gradient=gradient, basis=basis)


def reference(momentum, gradient, basis):
    width = math.gcd(FF, 1024)
    count = FF // width
    scale = math.sqrt(D * FF / RANK)

    def summed_cols(index):
        start = index * width
        left = lax.dynamic_slice_in_dim(momentum, start, width, 1).astype(jnp.float32)
        right = lax.dynamic_slice_in_dim(gradient, start, width, 1).astype(jnp.float32)
        return left + right

    def panel_step(index, total):
        block = summed_cols(index).astype(jnp.bfloat16)
        rows = lax.dynamic_slice_in_dim(basis, index * width, width, 0).astype(jnp.bfloat16)
        return total + jnp.dot(block.astype(jnp.float32), rows.astype(jnp.float32), preferred_element_type=jnp.float32)
    panel = lax.fori_loop(0, count, panel_step, jnp.zeros((D, RANK), jnp.float32))
    gram = jnp.dot(panel.T.astype(jnp.float32), panel.astype(jnp.float32), precision=lax.Precision.HIGHEST, preferred_element_type=jnp.float32)
    factor = jnp.linalg.cholesky(gram)
    ortho = lax.linalg.triangular_solve(factor, panel, left_side=False, lower=True, transpose_a=True).astype(jnp.bfloat16)

    def cross_block(index):
        block = summed_cols(index).astype(jnp.bfloat16)
        return jnp.dot(block.T.astype(jnp.float32), ortho.astype(jnp.float32), preferred_element_type=jnp.float32)
    indices = jnp.arange(count, dtype=jnp.int32)
    cross = lax.map(cross_block, indices).reshape(FF, RANK)
    colsq = lax.optimization_barrier(jnp.sum(cross * cross, axis=0))
    scaleinv = 1.0 / jnp.sqrt(colsq + 1e-06)
    cross_b = cross.astype(jnp.bfloat16)
    newbasis = (cross_b.astype(jnp.float32) * scaleinv).astype(jnp.bfloat16)

    def out_block(index):
        start = index * width
        summed = summed_cols(index)
        basis_rows = lax.dynamic_slice_in_dim(newbasis, start, width, 0)
        cross_rows = lax.dynamic_slice_in_dim(cross_b, start, width, 0)
        upd = (scale * jnp.dot(ortho.astype(jnp.float32), basis_rows.T.astype(jnp.float32), preferred_element_type=jnp.float32)).astype(jnp.bfloat16)
        mom = (summed - 0.05 * jnp.dot(ortho.astype(jnp.float32), cross_rows.T.astype(jnp.float32), preferred_element_type=jnp.float32)).astype(jnp.bfloat16)
        return (upd, mom)
    upd_blocks, mom_blocks = lax.map(out_block, indices)
    update = jnp.transpose(upd_blocks, (1, 0, 2)).reshape(D, FF)
    new_momentum = jnp.transpose(mom_blocks, (1, 0, 2)).reshape(D, FF)
    return (update, new_momentum)
```

```python
import functools
import math

import jax
import jax.numpy as jnp
from jax import lax
from jax.experimental import pallas as pl
from jax.experimental.pallas import tpu as pltpu
from jax.sharding import PartitionSpec as P

MESH = pl.DeviceIdType.MESH
HIGHEST = lax.Precision.HIGHEST
RANK = 128
NX = 4
NEAR = 8
FAR = 4
F32 = jnp.float32
BF16 = jnp.bfloat16


class Plan:
    def __init__(self, n_fsdp, n_tensor, rows, cols):
        self.nz, self.nx, self.nt = n_fsdp // NX, NX, n_tensor
        assert self.nz == NEAR * FAR
        self.rows, self.cols = rows, cols
        self.piece = cols // n_fsdp
        self.slot = -(-self.piece // 16) * 16
        self.block = self.piece * FAR
        self.sent = -(-self.block // 16) * 16
        self.near = [d for d in range(NEAR // 2, 0, -1)] + [-d for d in range((NEAR - 1) // 2, 0, -1)]
        self.near.sort(key=abs)
        self.strip = rows // n_tensor
        self.chunk = 256 if cols % 256 == 0 else cols // self.nx


class Copies:
    def __init__(self, send, recv):
        self.send, self.recv, self.used, self.out = send, recv, 0, []

    def start(self, src, dst, device):
        i = self.used
        self.used += 1
        copy = pltpu.make_async_remote_copy(
            src_ref=src, dst_ref=dst, send_sem=self.send.at[i], recv_sem=self.recv.at[i],
            device_id=device, device_id_type=MESH,
        )
        copy.start()
        self.out.append(copy)
        return copy

    def finish(self):
        for copy in self.out:
            copy.wait_send()


def n_copies(plan):
    near, far, x, t = len(plan.near), FAR - 1, plan.nx - 1, plan.nt - 1
    gather = far + near + NEAR * x
    total = gather + 2 * t + (near + far + x + t) + (NEAR * x + near + far) + gather + (near + far + x + t)
    return max(total, 1)


def factor(gp_ref, ot_ref):
    n = RANK
    lane = lax.broadcasted_iota(jnp.int32, (n, n), 1)
    lane1 = lax.broadcasted_iota(jnp.int32, (1, n), 1)
    row1 = lax.broadcasted_iota(jnp.int32, (n, 1), 0)

    def step(s, carry):
        j = s * 4
        gram = gp_ref[:, :n]
        cols, rows = [], []
        for p in range(4):
            rows.append(gp_ref[pl.ds(j + p, 1), :])
            cols.append(jnp.sum(jnp.where(lane == j + p, gram, 0.0), axis=1, keepdims=True))
        a = [[jnp.sum(jnp.where(lane1 == j + q, rows[p][:, :n], 0.0), axis=1, keepdims=True)
              for q in range(p + 1)] for p in range(4)]
        inv, mults = [], []
        for p in range(4):
            for q in range(p):
                low = a[p][q] * inv[q]
                rows[p] = rows[p] - low * rows[q]
                cols[p] = cols[p] - low * cols[q]
                for r in range(p, 4):
                    a[r][p] = a[r][p] - low * a[r][q]
            inv.append(1.0 / a[p][p])
            mults.append(jnp.where(row1 > j + 3, cols[p] * inv[p], 0.0))
            ot_ref[pl.ds(j + p, 1), :] = rows[p][:, n:] * (1.0 / jnp.sqrt(a[p][p]))
        new = gp_ref[...]
        for p in range(4):
            new = new - mults[p] * rows[p]
        gp_ref[...] = new
        return carry

    lax.fori_loop(0, n // 4, step, 0)


def kernel(plan, m_ref, g_ref, b_ref, ortho_ref, piece_ref, newb_ref,
           sb, basis_buf, tile, basis32, part, part_in, strip, panel, gram, gram_x, gram_n, gram_f, gram_t,
           strip_x, strip_n, strip_f, gp, ot,
           cross, cross_x, sum_x, cross_n, sum_n, cross_f, cross_buf, nat,
           sq, sq_f, sq_n, sq_x, sq_t, send_sem, recv_sem):
    f, t = lax.axis_index("fsdp"), lax.axis_index("tensor")
    nz, nx, nt = plan.nz, plan.nx, plan.nt
    z, x = f // nx, f % nx
    near_id, far_id = z % NEAR, z // NEAR
    comm = Copies(send_sem, recv_sem)

    def at_z(d):
        return (lax.rem(z + d + nz, nz) * nx + x, t)

    def at_x(d):
        return (z * nx + lax.rem(x + d, nx), t)

    def at_t(d):
        return (f, lax.rem(t + d, nt))

    barrier = pltpu.get_barrier_semaphore()
    peers = [at_z(NEAR * d) for d in range(1, FAR)] + [at_z(-d) for d in plan.near]
    peers += [at_x(d) for d in range(1, nx)] + [at_t(d) for d in range(1, nt)]
    for device in peers:
        pl.semaphore_signal(barrier, inc=1, device_id=device, device_id_type=MESH)

    basis_buf[x, near_id, far_id, 0:plan.slot] = jnp.zeros((plan.slot, RANK), BF16)
    basis_buf[x, near_id, far_id, 0:plan.piece] = b_ref[...].astype(BF16)
    chunk = plan.chunk
    n_chunks = plan.cols // chunk

    def add(i, carry):
        c = pl.ds(pl.multiple_of(i * chunk, chunk), chunk)
        sb[:, c] = (m_ref[:, c].astype(F32) + g_ref[:, c].astype(F32)).astype(BF16)
        return carry

    lax.fori_loop(0, n_chunks, add, 0)
    pl.semaphore_wait(barrier, len(peers))

    def spread(buf, view, wait_first=()):
        def forward(near):
            block = view(x, near)
            return [comm.start(block, block, at_x(d)) for d in range(1, nx)]

        block = view(x, near_id)
        zs = [comm.start(block, block, at_z(d)) for d in plan.near]
        return forward, zs

    own = basis_buf.at[x, near_id, far_id]
    for copy in [comm.start(own, own, at_z(NEAR * d)) for d in range(1, FAR)]:
        copy.wait_recv()
    forward, zs = spread(basis_buf, lambda xx, nn: basis_buf.at[xx, nn])
    xs = forward(near_id)
    for d, copy in zip(plan.near, zs):
        copy.wait_recv()
        xs += forward(lax.rem(near_id - d + NEAR, NEAR))
    for copy in xs:
        copy.wait_recv()

    def unpack(zz, carry):
        for xx in range(nx):
            tile[xx * plan.piece:(xx + 1) * plan.piece, :] = basis_buf[
                xx, zz % NEAR, zz // NEAR, 0:plan.piece].astype(F32)
        n = nx * plan.piece
        basis32[pl.ds(pl.multiple_of(zz * n, 8), n), :] = tile[...]
        return carry

    lax.fori_loop(0, nz, unpack, 0)
    part[...] = jnp.zeros_like(part)

    def multiply(i, carry):
        c = pl.ds(pl.multiple_of(i * chunk, chunk), chunk)
        part[...] += jnp.dot(sb[:, c], basis32[c, :].astype(BF16), preferred_element_type=F32)
        return carry

    lax.fori_loop(0, n_chunks, multiply, 0)

    w = plan.strip

    def strip_of(ref, i):
        return ref.at[pl.ds(pl.multiple_of(i * w, w), w)]

    got = [comm.start(strip_of(part, lax.rem(t + d, nt)), part_in.at[d], at_t(d)) for d in range(1, nt)]
    total = strip_of(part, t)[...]
    for d, copy in zip(range(1, nt), got):
        copy.wait_recv()
        total = total + part_in[d]
    strip_of(panel, t)[...] = total
    mine = strip_of(panel, t)
    got = [comm.start(mine, mine, at_t(d)) for d in range(1, nt)]
    for copy in got:
        copy.wait_recv()

    pan = panel[...]
    gram[...] = lax.dot_general(
        pan, pan, (((0,), (0,)), ((), ())), precision=HIGHEST, preferred_element_type=F32)
    strip[...] = strip_of(gram, t)[...]

    def reduce(src, slots, out, devices):
        got = [comm.start(src, slots.at[i], device) for i, device in enumerate(devices)]
        total = src[...]
        for i, copy in enumerate(got):
            copy.wait_recv()
            total = total + slots[i]
        out[...] = total

    x_devices = [at_x(d) for d in range(1, nx)]
    near_devices = [at_z(d) for d in plan.near]
    far_devices = [at_z(NEAR * d) for d in range(1, FAR)]
    reduce(strip, gram_x, strip_x, x_devices)
    reduce(strip_x, gram_n, strip_n, near_devices)
    reduce(strip_n, gram_f, strip_f, far_devices)
    mine = strip_of(gram_t, t)
    mine[...] = strip_f[...]
    got = [comm.start(mine, mine, at_t(d)) for d in range(1, nt)]
    gp[:, RANK:] = pan.T
    for copy in got:
        copy.wait_recv()
    gp[:, :RANK] = gram_t[...]

    factor(gp, ot)
    ortho = ot[...].T.astype(BF16)
    ortho_ref[...] = ortho

    def cross_chunk(i, carry):
        c = pl.ds(pl.multiple_of(i * chunk, chunk), chunk)
        cross[c, :] = lax.dot_general(
            sb[:, c], ortho, (((0,), (0,)), ((), ())), preferred_element_type=F32)
        return carry

    lax.fori_loop(0, n_chunks, cross_chunk, 0)

    block, per_x = plan.block, plan.block * NEAR

    def rows_of(xx, near):
        return pl.ds(pl.multiple_of(xx * per_x + near * block, 8), block)

    order = plan.near[::-1] + [0]
    got = []
    for o, d in enumerate(order):
        near = lax.rem(near_id + d + NEAR, NEAR)
        got.append([comm.start(cross.at[rows_of(lax.rem(x + dx, nx), near)], cross_x.at[dx - 1, o], at_x(dx))
                    for dx in range(1, nx)])
    sum_n[...] = jnp.zeros_like(sum_n)
    zs = []
    for o, d in enumerate(order):
        near = lax.rem(near_id + d + NEAR, NEAR)
        total = cross[rows_of(x, near), :]
        for dx, copy in enumerate(got[o]):
            copy.wait_recv()
            total = total + cross_x[dx, o]
        if d:
            sum_x[o] = total
            zs.append(comm.start(sum_x.at[o], cross_n.at[o], at_z(d)))
        else:
            for i, copy in enumerate(zs):
                copy.wait_recv()
                total = total + cross_n[i]
            sum_n[0:block, :] = total
    slot = plan.slot

    def slot_rows(i):
        return pl.ds(pl.multiple_of(i * slot, slot), slot)

    got = [comm.start(sum_n.at[slot_rows(lax.rem(far_id + d, FAR))], cross_f.at[d - 1], at_z(NEAR * d))
           for d in range(1, FAR)]
    total = sum_n[slot_rows(far_id), :]
    for i, copy in enumerate(got):
        copy.wait_recv()
        total = total + cross_f[i]

    sq[0] = jnp.broadcast_to(jnp.sum(total * total, axis=0, keepdims=True), (8, RANK))
    own = cross_buf.at[x, near_id, slot_rows(far_id)]
    own[...] = total.astype(BF16)
    got = [comm.start(own, own, device) for device in far_devices]
    reduce(sq.at[0], sq_f, sq.at[1], far_devices)
    for copy in got:
        copy.wait_recv()
    forward, zs = spread(cross_buf, lambda xx, nn: cross_buf.at[xx, nn, pl.ds(0, plan.sent)])
    reduce(sq.at[1], sq_n, sq.at[2], near_devices)
    reduce(sq.at[2], sq_x, sq.at[3], x_devices)
    got = [comm.start(sq.at[3], sq_t.at[d - 1], at_t(d)) for d in range(1, nt)]
    xs = forward(near_id)
    for d, copy in zip(plan.near, zs):
        copy.wait_recv()
        xs += forward(lax.rem(near_id - d + NEAR, NEAR))
    total = sq[3]
    for i, copy in enumerate(got):
        copy.wait_recv()
        total = total + sq_t[i]
    scaleinv = 1.0 / jnp.sqrt(total[0:1, :] + 1e-06)
    for copy in xs:
        copy.wait_recv()

    def settle(i, carry):
        nat[pl.ds(pl.multiple_of(i * block, 8), block), :] = cross_buf[
            i // NEAR, i % NEAR, 0:block].astype(F32)
        return carry

    lax.fori_loop(0, nx * NEAR, settle, 0)

    def scale_rows(i, carry):
        c = pl.ds(pl.multiple_of(i * chunk, 16), chunk)
        value = nat[c, :]
        piece_ref[c, :] = value.astype(BF16)
        newb_ref[c, :] = (value * scaleinv).astype(BF16)
        return carry

    lax.fori_loop(0, n_chunks, scale_rows, 0)
    comm.finish()


def exchange(plan, momentum, gradient, basis):
    nx, nt, near, far = plan.nx, plan.nt, max(len(plan.near), 1), FAR - 1
    vmem = pl.BlockSpec(memory_space=pltpu.VMEM)
    w = plan.strip
    scratch = [
        pltpu.VMEM((plan.rows, plan.cols), BF16),
        pltpu.VMEM((nx, NEAR, FAR, plan.slot, RANK), BF16),
        pltpu.VMEM((nx * plan.piece, RANK), F32),
        pltpu.VMEM((plan.cols, RANK), F32),
        pltpu.VMEM((plan.rows, RANK), F32),
        pltpu.VMEM((nt, w, RANK), F32),
        pltpu.VMEM((w, RANK), F32),
        pltpu.VMEM((plan.rows, RANK), F32),
        pltpu.VMEM((RANK, RANK), F32),
        pltpu.VMEM((nx - 1, w, RANK), F32),
        pltpu.VMEM((near, w, RANK), F32),
        pltpu.VMEM((far, w, RANK), F32),
        pltpu.VMEM((RANK, RANK), F32),
        pltpu.VMEM((w, RANK), F32),
        pltpu.VMEM((w, RANK), F32),
        pltpu.VMEM((w, RANK), F32),
        pltpu.VMEM((RANK, RANK + plan.rows), F32),
        pltpu.VMEM((RANK, plan.rows), F32),
        pltpu.VMEM((plan.cols, RANK), F32),
        pltpu.VMEM((nx - 1, NEAR, plan.block, RANK), F32),
        pltpu.VMEM((near, plan.block, RANK), F32),
        pltpu.VMEM((near, plan.block, RANK), F32),
        pltpu.VMEM((FAR * plan.slot, RANK), F32),
        pltpu.VMEM((far, plan.slot, RANK), F32),
        pltpu.VMEM((nx, NEAR, FAR * plan.slot, RANK), BF16),
        pltpu.VMEM((plan.cols, RANK), F32),
        pltpu.VMEM((4, 8, RANK), F32),
        pltpu.VMEM((far, 8, RANK), F32),
        pltpu.VMEM((near, 8, RANK), F32),
        pltpu.VMEM((nx - 1, 8, RANK), F32),
        pltpu.VMEM((max(nt - 1, 1), 8, RANK), F32),
        pltpu.SemaphoreType.DMA((n_copies(plan),)),
        pltpu.SemaphoreType.DMA((n_copies(plan),)),
    ]
    return pl.pallas_call(
        functools.partial(kernel, plan),
        out_shape=(
            jax.ShapeDtypeStruct((plan.rows, RANK), BF16),
            jax.ShapeDtypeStruct((plan.cols, RANK), BF16),
            jax.ShapeDtypeStruct((plan.cols, RANK), BF16),
        ),
        in_specs=[vmem] * 3,
        out_specs=(vmem,) * 3,
        scratch_shapes=scratch,
        compiler_params=pltpu.CompilerParams(
            collective_id=0, has_side_effects=True, vmem_limit_bytes=48 * 1024 * 1024),
        cost_estimate=pl.CostEstimate(
            flops=4 * plan.rows * plan.cols * RANK, bytes_accessed=6 * plan.rows * plan.cols, transcendentals=0),
        name="dion_exchange",
    )(momentum, gradient, basis)


def solution(mesh):
    n_fsdp, n_tensor = mesh.shape["fsdp"], mesh.shape["tensor"]

    def body(momentum, gradient, basis):
        rows, cols = momentum.shape
        plan = Plan(n_fsdp, n_tensor, rows, cols)
        scale = math.sqrt(rows * n_fsdp * cols * n_tensor / RANK)
        ortho, piece, newbasis = exchange(plan, momentum, gradient, basis)
        dims = (((1,), (1,)), ((), ()))
        update = scale * lax.dot_general(ortho, newbasis, dims, preferred_element_type=F32)
        summed = momentum.astype(F32) + gradient.astype(F32)
        moved = summed - 0.05 * lax.dot_general(ortho, piece, dims, preferred_element_type=F32)
        return update.astype(BF16), moved.astype(BF16)

    in_specs = (P("fsdp", "tensor"), P("fsdp", "tensor"), P(("tensor", "fsdp"), None))
    out_specs = (P("fsdp", "tensor"), P("fsdp", "tensor"))
    return jax.shard_map(body, mesh=mesh, in_specs=in_specs, out_specs=out_specs, check_vma=False)
```

```python
import functools
import math

import jax
import jax.numpy as jnp
from jax import lax
from jax.experimental import pallas as pl
from jax.experimental.pallas import tpu as pltpu
from jax.sharding import PartitionSpec as P

MESH = pl.DeviceIdType.MESH
HIGHEST = lax.Precision.HIGHEST
RANK = 128
NX = 4
NEAR = 8
FAR = 4
CORES = 2
F32 = jnp.float32
BF16 = jnp.bfloat16


class Plan:
    def __init__(self, n_fsdp, n_tensor, rows, cols):
        self.nz, self.nx, self.nt, self.ny = n_fsdp // NX, NX, n_tensor, n_tensor // CORES
        assert self.nz == NEAR * FAR and NX == 4
        self.rows, self.cols = rows, cols
        self.piece = cols // n_fsdp
        self.slot = -(-self.piece // 16) * 16
        self.block = self.piece * FAR
        self.sent = -(-self.block // 16) * 16
        self.group = self.block * NX
        self.near = sorted([d for d in range(-((NEAR - 1) // 2), NEAR // 2 + 1) if d], key=abs)
        self.far = [(2 * i + 1) * (NEAR // 2) for i in range(-(FAR // 2), FAR // 2)]
        self.far.sort(key=abs, reverse=True)
        self.strip = RANK // n_tensor
        self.chunk = 256 if cols % 256 == 0 else cols // self.nx
        self.batches = [(a, b) for a, b in ((0, 1), (1, NEAR // 2 + 1), (NEAR // 2 + 1, NEAR)) if a < b]


class Copies:
    def __init__(self, send, recv):
        self.send, self.recv, self.used, self.out = send, recv, 0, []

    def start(self, src, dst, device):
        i = self.used
        self.used += 1
        copy = pltpu.make_async_remote_copy(
            src_ref=src, dst_ref=dst, send_sem=self.send.at[i], recv_sem=self.recv.at[i],
            device_id=device, device_id_type=MESH,
        )
        copy.start()
        self.out.append(copy)
        return copy

    def drain(self, keep=0):
        n = len(self.out) - keep
        for copy in self.out[:n]:
            copy.wait_send()
        self.out = self.out[n:]


def n_copies(plan):
    near, far, x, y = len(plan.near), len(plan.far), plan.nx - 1, plan.ny - 1
    gather = far + near + x * len(plan.batches)
    return 2 * gather + (y + 2) + (x + near + far + y + 1) + (2 * NEAR + near + far) + (far + near + x + y + 1)


def factor(gp_ref, ot_ref):
    n, nb = RANK, 32
    lane1 = lax.broadcasted_iota(jnp.int32, (1, n), 1)
    for top in range(0, n, nb):
        lane = lax.broadcasted_iota(jnp.int32, (n - top, n), 1)
        row1 = lax.broadcasted_iota(jnp.int32, (n - top, 1), 0) + top

        def step(s, carry, top=top, lane=lane, row1=row1):
            j = top + s * 4
            gram = gp_ref[top:, :n]
            cols, rows = [], []
            for p in range(4):
                rows.append(gp_ref[pl.ds(j + p, 1), :])
                cols.append(jnp.sum(jnp.where(lane == j + p, gram, 0.0), axis=1, keepdims=True))
            a = [[jnp.sum(jnp.where(lane1 == j + q, rows[p][:, :n], 0.0), axis=1, keepdims=True)
                  for q in range(p + 1)] for p in range(4)]
            inv, mults = [], []
            for p in range(4):
                for q in range(p):
                    low = a[p][q] * inv[q]
                    rows[p] = rows[p] - low * rows[q]
                    cols[p] = cols[p] - low * cols[q]
                    for r in range(p, 4):
                        a[r][p] = a[r][p] - low * a[r][q]
                inv.append(1.0 / a[p][p])
                mults.append(jnp.where(row1 > j + 3, cols[p] * inv[p], 0.0))
                ot_ref[pl.ds(j + p, 1), :] = rows[p][:, n:] * (1.0 / jnp.sqrt(a[p][p]))
            new = gp_ref[top:, :]
            for p in range(4):
                new = new - mults[p] * rows[p]
            gp_ref[top:, :] = new
            return carry

        lax.fori_loop(0, nb // 4, step, 0)


def kernel(plan, m_hbm, g_hbm, b_ref, ortho_ref, piece_ref, scale_ref,
           m_ref, g_ref, turned, turned_b, lines, tiles, spread, basis_own, basis_in, packed, basis_buf,
           part, part_c, part_y, panel, strip, gram_x, gram_n, gram_f, gram_t, gp, ot,
           cross, cross_r, cross_x, sum_x, cross_n, sum_n, cross_f, cross_own, cross_held, cross_buf, nat,
           sq, sq_f, sq_n, sq_x, sq_y, sq_c, send_sem, recv_sem, load_sem):
    f, t = lax.axis_index("fsdp"), lax.axis_index("tensor")
    nz, nx, ny = plan.nz, plan.nx, plan.ny
    z, x = f // nx, f % nx
    y, core = t // CORES, t % CORES
    near_id, far_id = z % NEAR, z // NEAR
    comm = Copies(send_sem, recv_sem)

    def at_z(d):
        return (lax.rem(z + d + nz, nz) * nx + x, t)

    x_devices = [(z * nx + lax.rem(x + d, nx), t) for d in (2, 1, 3)]
    y_devices = [(f, lax.rem(y + d, ny) * CORES + core) for d in range(1, ny)]
    sibling = (f, y * CORES + 1 - core)
    right, across, left = (lax.rem(x + d, nx) for d in (1, 2, 3))
    to_right, to_left = x_devices[1], x_devices[2]
    near_devices = [at_z(d) for d in plan.near]
    far_devices = [at_z(d) for d in plan.far]

    loads = [pltpu.make_async_copy(m_hbm, m_ref, load_sem.at[0]), pltpu.make_async_copy(g_hbm, g_ref, load_sem.at[1])]
    for load in loads:
        load.start()
    barrier = pltpu.get_barrier_semaphore()
    peers = far_devices + [at_z(-d) for d in plan.near] + x_devices + y_devices + [sibling]
    for device in peers:
        pl.semaphore_signal(barrier, inc=1, device_id=device, device_id_type=MESH)

    basis_own[...] = jnp.zeros_like(basis_own)
    basis_own[0:plan.piece, :] = b_ref[...].astype(BF16)
    chunk = plan.chunk
    for load in loads:
        load.wait()

    def turn(i, carry):
        c = pl.ds(pl.multiple_of(i * chunk, chunk), chunk)
        value = (m_ref[:, c].astype(F32) + g_ref[:, c].astype(F32)).astype(BF16).astype(F32).T
        turned[c, :] = value
        turned_b[c, :] = value.astype(BF16)
        return carry

    lax.fori_loop(0, plan.cols // chunk, turn, 0)
    tiles[...] = jnp.zeros_like(tiles)
    packed[...] = jnp.zeros_like(packed)
    pl.semaphore_wait(barrier, len(peers))

    def begin(src, slots, devices):
        return [comm.start(src, slots.at[i], device) for i, device in enumerate(devices)]

    def add_up(total, slots, copies):
        for i, copy in enumerate(copies):
            copy.wait_recv()
            total = slots[i] if total is None else total + slots[i]
        return total

    def gathered(near):
        return lax.rem(near_id - near + NEAR + NEAR // 2, NEAR)

    slot = basis_in.at[far_id]
    far_copies = [comm.start(basis_own, slot, device) for device in far_devices]
    piece = plan.piece

    def space(i, carry):
        for k in range(FAR):
            n = nx * piece
            lines[...] = turned[pl.ds(pl.multiple_of((i + NEAR * k) * n, 8), n), :]
            for xx in range(nx):
                tiles[xx, k * piece:(k + 1) * piece, :] = lines[xx * piece:(xx + 1) * piece, :]
        for xx in range(nx):
            spread[xx, i] = tiles[xx].T.astype(BF16)
        return carry

    lax.fori_loop(0, NEAR, space, 0)
    for copy in far_copies:
        copy.wait_recv()
    for k in range(FAR):
        packed[k * piece:(k + 1) * piece, :] = basis_in[k, 0:piece].astype(F32)
    basis_buf[x, 0:plan.sent] = packed[...].astype(BF16)

    shifts = [0] + plan.near

    def pass_on(buf, before_batch=None):
        n = plan.sent
        block = buf.at[x, pl.ds(0, n)]
        z_copies = [comm.start(block, buf.at[x, pl.ds((i + 1) * n, n)], near_devices[i])
                    for i in reversed(range(NEAR - 1))][::-1]
        sent = []
        for a, b in plan.batches:
            for i in range(max(a, 1), b):
                z_copies[i - 1].wait_recv()
            blocks = buf.at[x, pl.ds(a * n, (b - a) * n)]
            sent.append([comm.start(blocks, blocks, device) for device in x_devices])
            if before_batch is not None:
                before_batch(a)
        return sent

    total = jnp.zeros((plan.rows, RANK), F32)
    for (a, b), copies in zip(plan.batches, pass_on(basis_buf)):
        for copy in copies:
            copy.wait_recv()
        for i in range(a, b):
            near = gathered(shifts[i])
            for xx in range(nx):
                total = total + jnp.dot(spread[xx, near][:, :plan.sent],
                                        basis_buf[xx, i * plan.sent:(i + 1) * plan.sent], preferred_element_type=F32)
    part[...] = total

    def half_of(ref, i):
        n = plan.rows // CORES
        return ref.at[pl.ds(pl.multiple_of(i * n, n), n)]

    comm.start(half_of(part, 1 - core), part_c, sibling).wait_recv()
    part_y[y] = half_of(part, core)[...] + part_c[...]
    for copy in [comm.start(part_y.at[y], part_y.at[y], device) for device in y_devices]:
        copy.wait_recv()
    mine = half_of(panel, core)
    total = part_y[0]
    for i in range(1, ny):
        total = total + part_y[i]
    mine[...] = total
    comm.start(mine, mine, sibling).wait_recv()

    w = plan.strip

    def strip_of(ref):
        return ref.at[pl.ds(pl.multiple_of((core * ny + y) * w, w), w)]

    pan = panel[...]
    gp[:, RANK:] = pan.T
    lines_t = gp[pl.ds(pl.multiple_of((core * ny + y) * w, w), w), RANK:]
    strip[0] = jnp.dot(lines_t, pan, precision=HIGHEST, preferred_element_type=F32)
    strip[1] = add_up(strip[0], gram_x, begin(strip.at[0], gram_x, x_devices))
    strip[2] = add_up(strip[1], gram_n, begin(strip.at[1], gram_n, near_devices[::-1]))
    copies = begin(strip.at[2], gram_f, far_devices)
    comm.drain(keep=FAR)
    mine = strip_of(gram_t)
    mine[...] = add_up(None, gram_f, copies)
    for copy in [comm.start(mine, mine, device) for device in y_devices]:
        copy.wait_recv()
    mine = half_of(gram_t, core)
    comm.start(mine, mine, sibling).wait_recv()
    gp[:, :RANK] = gram_t[...]

    factor(gp, ot)
    ortho = ot[...].T.astype(BF16)
    ortho_ref[...] = ortho

    rows, group = plan.block, plan.group
    order = plan.near[::-1] + [0]
    pairs = [(o, o + 1) for o in range(0, NEAR, 2)]
    z_copies = []
    sum_n[...] = jnp.zeros_like(sum_n)

    def send_x(pair):
        for o in pair:
            first = lax.rem(near_id + order[o] + NEAR + NEAR // 2, NEAR) * group
            value = jnp.dot(turned_b[pl.ds(pl.multiple_of(first, 16), group), :], ortho, preferred_element_type=F32)
            for xx in range(nx):
                cross[xx, o] = value[xx * rows:(xx + 1) * rows, :]
        a, b = pair
        return [comm.start(cross.at[across, a], cross_r.at[0, a], to_right),
                comm.start(cross.at[across, b], cross_r.at[1, a], to_left)]

    def pass_x(pair, copies):
        a, b = pair
        for copy in copies:
            copy.wait_recv()
        cross[right, a] += cross_r[0, a]
        cross[left, b] += cross_r[1, a]
        return [comm.start(cross.at[xx, pl.ds(a, 2)], cross_x.at[i, pl.ds(a, 2)], device)
                for i, (xx, device) in enumerate(((right, to_right), (left, to_left)))]

    def add_x(pair, copies):
        for copy in copies:
            copy.wait_recv()
        for o in pair:
            total = cross[x, o] + cross_x[0, o] + cross_x[1, o]
            if order[o]:
                sum_x[o] = total
                z_copies.append(comm.start(sum_x.at[o], cross_n.at[o], at_z(order[o])))
            else:
                sum_n[0:rows, :] = add_up(total, cross_n, z_copies)

    first, second = [], []
    for i in range(len(pairs) + 2):
        if i < len(pairs):
            first.append(send_x(pairs[i]))
        if 1 <= i <= len(pairs):
            second.append(pass_x(pairs[i - 1], first[i - 1]))
        if i >= 2:
            add_x(pairs[i - 2], second[i - 2])

    def far_rows(i):
        return pl.ds(pl.multiple_of(i * plan.slot, plan.slot), plan.slot)

    copies = [comm.start(sum_n.at[far_rows(lax.rem(z + d + nz, nz) // NEAR)], cross_f.at[i], device)
              for i, (d, device) in enumerate(zip(plan.far, far_devices))]
    comm.drain(keep=FAR)
    total = add_up(None, cross_f, copies)

    cross_own[...] = total.astype(BF16)
    slot = cross_held.at[far_rows(far_id)]
    far_copies = [comm.start(cross_own, slot, device) for device in far_devices]
    sq[0] = jnp.broadcast_to(jnp.sum(total * total, axis=0, keepdims=True), (8, RANK))
    sq_copies = begin(sq.at[0], sq_f, far_devices)
    comm.drain(keep=2 * FAR)
    for copy in far_copies:
        copy.wait_recv()
    cross_buf[x, 0:plan.sent] = cross_held[0:plan.sent, :]
    sq[1] = add_up(None, sq_f, sq_copies)
    sq_copies = begin(sq.at[1], sq_n, near_devices)

    def before_batch(a):
        if a == 0:
            sq[2] = add_up(sq[1], sq_n, sq_copies)
            later.append(begin(sq.at[2], sq_x, x_devices))

    later = []
    batches = list(zip(plan.batches, pass_on(cross_buf, before_batch)))
    sq[3] = add_up(sq[2], sq_x, later[0])
    sq_copies = begin(sq.at[3], sq_y, y_devices)

    def settle(batch):
        (a, b), copies = batch
        for copy in copies:
            copy.wait_recv()
        for i in range(a, b):
            for xx in range(nx):
                nat[xx * rows:(xx + 1) * rows, :] = cross_buf[xx, i * plan.sent:i * plan.sent + rows].astype(F32)
            first = pl.multiple_of(gathered(shifts[i]) * group, 16)
            piece_ref[pl.ds(first, group), :] = nat[...].astype(BF16)

    for batch in batches[:-1]:
        settle(batch)
    sq[4] = add_up(sq[3], sq_y, sq_copies)
    last = comm.start(sq.at[4], sq_c.at[0], sibling)
    settle(batches[-1])
    scale_ref[...] = 1.0 / jnp.sqrt(add_up(sq[4], sq_c, [last]) + 1e-06)
    comm.drain()


def exchange(plan, momentum, gradient, basis):
    nx, ny, near, far = plan.nx, plan.ny, len(plan.near), len(plan.far)
    w, half = plan.strip, plan.rows // CORES

    def f32(*shape):
        return pltpu.VMEM((*shape, RANK), F32)

    def bf16(*shape):
        return pltpu.VMEM((*shape, RANK), BF16)

    whole = pltpu.VMEM((plan.rows, plan.cols), BF16)
    scratch = [
        whole, whole, f32(plan.cols), bf16(plan.cols), f32(nx * plan.piece), f32(nx, FAR * plan.slot),
        pltpu.VMEM((nx, NEAR, plan.rows, FAR * plan.slot), BF16), bf16(plan.slot), bf16(FAR, plan.slot),
        f32(plan.sent), bf16(nx, NEAR * plan.sent),
        f32(plan.rows), f32(half), f32(ny, half), f32(plan.rows), f32(3, w),
        f32(nx - 1, w), f32(near, w), f32(far, w), f32(RANK),
        pltpu.VMEM((RANK, RANK + plan.rows), F32), pltpu.VMEM((RANK, plan.rows), F32),
        f32(nx, NEAR, plan.block), f32(2, NEAR, plan.block), f32(2, NEAR, plan.block), f32(near, plan.block), f32(near, plan.block),
        f32(FAR * plan.slot), f32(far, plan.slot), bf16(plan.slot), bf16(FAR * plan.slot), bf16(nx, NEAR * plan.sent),
        f32(plan.group),
        f32(5, 8), f32(far, 8), f32(near, 8), f32(nx - 1, 8), f32(max(ny - 1, 1), 8), f32(1, 8),
        pltpu.SemaphoreType.DMA((n_copies(plan),)),
        pltpu.SemaphoreType.DMA((n_copies(plan),)),
        pltpu.SemaphoreType.DMA((2,)),
    ]
    vmem, hbm = pl.BlockSpec(memory_space=pltpu.VMEM), pl.BlockSpec(memory_space=pl.ANY)
    return pl.pallas_call(
        functools.partial(kernel, plan),
        out_shape=(
            jax.ShapeDtypeStruct((plan.rows, RANK), BF16),
            jax.ShapeDtypeStruct((plan.cols, RANK), BF16),
            jax.ShapeDtypeStruct((8, RANK), F32),
        ),
        in_specs=[hbm, hbm, vmem],
        out_specs=(vmem,) * 3,
        scratch_shapes=scratch,
        compiler_params=pltpu.CompilerParams(
            collective_id=0, has_side_effects=True, vmem_limit_bytes=56 * 1024 * 1024),
        cost_estimate=pl.CostEstimate(
            flops=4 * plan.rows * plan.cols * RANK, bytes_accessed=6 * plan.rows * plan.cols, transcendentals=0),
        name="dion_exchange",
    )(momentum, gradient, basis)


def solution(mesh):
    n_fsdp, n_tensor = mesh.shape["fsdp"], mesh.shape["tensor"]

    def body(momentum, gradient, basis):
        rows, cols = momentum.shape
        plan = Plan(n_fsdp, n_tensor, rows, cols)
        scale = math.sqrt(rows * n_fsdp * cols * n_tensor / RANK)
        ortho, piece, scaleinv = exchange(plan, momentum, gradient, basis)
        newbasis = (piece.astype(F32) * scaleinv[0:1]).astype(BF16)
        dims = (((1,), (1,)), ((), ()))
        update = scale * lax.dot_general(ortho, newbasis, dims, preferred_element_type=F32)
        summed = momentum.astype(F32) + gradient.astype(F32)
        moved = summed - 0.05 * lax.dot_general(ortho, piece, dims, preferred_element_type=F32)
        return update.astype(BF16), moved.astype(BF16)

    in_specs = (P("fsdp", "tensor"), P("fsdp", "tensor"), P(("tensor", "fsdp"), None))
    out_specs = (P("fsdp", "tensor"), P("fsdp", "tensor"))
    return jax.shard_map(body, mesh=mesh, in_specs=in_specs, out_specs=out_specs, check_vma=False)
```

```python
import functools
import math

import jax
import jax.numpy as jnp
from jax import lax
from jax.experimental import pallas as pl
from jax.experimental.pallas import tpu as pltpu
from jax.sharding import PartitionSpec as P

MESH = pl.DeviceIdType.MESH
HIGHEST = lax.Precision.HIGHEST
RANK = 128
NX = 4
NEAR = 8
FAR = 4
CORES = 2
F32 = jnp.float32
BF16 = jnp.bfloat16


class Plan:
    def __init__(self, n_fsdp, n_tensor, rows, cols):
        self.nz, self.nx, self.nt, self.ny = n_fsdp // NX, NX, n_tensor, n_tensor // CORES
        assert self.nz == NEAR * FAR and NX == 4
        self.rows, self.cols = rows, cols
        self.piece = cols // n_fsdp
        self.slot = -(-self.piece // 16) * 16
        self.block = self.piece * FAR
        self.sent = -(-self.block // 16) * 16
        self.group = self.block * NX
        self.near = sorted([d for d in range(-((NEAR - 1) // 2), NEAR // 2 + 1) if d], key=abs)
        self.far = [(2 * i + 1) * (NEAR // 2) for i in range(-(FAR // 2), FAR // 2)]
        self.far.sort(key=abs, reverse=True)
        self.strip = RANK // n_tensor
        self.chunk = 256 if cols % 256 == 0 else cols // self.nx
        edges = [0] + [e for e in (1, 3, 5) if e < NEAR] + [NEAR]
        self.batches = list(zip(edges, edges[1:]))


class Copies:
    def __init__(self, send, recv):
        self.send, self.recv, self.used, self.out = send, recv, 0, []

    def start(self, src, dst, device):
        i = self.used
        self.used += 1
        copy = pltpu.make_async_remote_copy(
            src_ref=src, dst_ref=dst, send_sem=self.send.at[i], recv_sem=self.recv.at[i],
            device_id=device, device_id_type=MESH,
        )
        copy.start()
        self.out.append(copy)
        return copy

    def drain(self, keep=0):
        n = len(self.out) - keep
        for copy in self.out[:n]:
            copy.wait_send()
        self.out = self.out[n:]


def n_copies(plan):
    near, far, x, y = len(plan.near), len(plan.far), plan.nx - 1, plan.ny - 1
    gather = far + near + x * len(plan.batches)
    return 2 * gather + (y + 2) + (2 * x + 1 + near + far + y + 1) + (2 * NEAR + near + far) + (far + near + x + y + 1)


def factor(gp_ref, ot_ref):
    n, nb = RANK, 32
    lane1 = lax.broadcasted_iota(jnp.int32, (1, n), 1)
    for top in range(0, n, nb):
        lane = lax.broadcasted_iota(jnp.int32, (n - top, n), 1)
        row1 = lax.broadcasted_iota(jnp.int32, (n - top, 1), 0) + top

        def step(s, carry, top=top, lane=lane, row1=row1):
            j = top + s * 4
            gram = gp_ref[top:, :n]
            cols, rows = [], []
            for p in range(4):
                rows.append(gp_ref[pl.ds(j + p, 1), :])
                cols.append(jnp.sum(jnp.where(lane == j + p, gram, 0.0), axis=1, keepdims=True))
            a = [[jnp.sum(jnp.where(lane1 == j + q, rows[p][:, :n], 0.0), axis=1, keepdims=True)
                  for q in range(p + 1)] for p in range(4)]
            inv, mults = [], []
            for p in range(4):
                for q in range(p):
                    low = a[p][q] * inv[q]
                    rows[p] = rows[p] - low * rows[q]
                    cols[p] = cols[p] - low * cols[q]
                    for r in range(p, 4):
                        a[r][p] = a[r][p] - low * a[r][q]
                inv.append(1.0 / a[p][p])
                mults.append(jnp.where(row1 > j + 3, cols[p] * inv[p], 0.0))
                ot_ref[pl.ds(j + p, 1), :] = rows[p][:, n:] * (1.0 / jnp.sqrt(a[p][p]))
            new = gp_ref[top:, :]
            for p in range(4):
                new = new - mults[p] * rows[p]
            gp_ref[top:, :] = new
            return carry

        lax.fori_loop(0, nb // 4, step, 0)


def kernel(plan, m_hbm, g_hbm, b_ref, ortho_ref, piece_ref, scale_ref,
           m_ref, g_ref, turned, turned_b, lines, tiles, spread, basis_own, basis_in, packed, basis_buf,
           part, part_c, part_y, panel, half_t, halves, strip, gram_x, gram_n, gram_f, gram_t, gp, ot,
           cross, cross_r, cross_x, sum_x, cross_n, sum_n, cross_f, cross_own, cross_held, cross_buf, nat,
           sq, sq_f, sq_n, sq_x, sq_y, sq_c, send_sem, recv_sem, load_sem):
    f, t = lax.axis_index("fsdp"), lax.axis_index("tensor")
    nz, nx, ny = plan.nz, plan.nx, plan.ny
    z, x = f // nx, f % nx
    y, core = t // CORES, t % CORES
    near_id, far_id = z % NEAR, z // NEAR
    comm = Copies(send_sem, recv_sem)

    def at_z(d):
        return (lax.rem(z + d + nz, nz) * nx + x, t)

    x_devices = [(z * nx + lax.rem(x + d, nx), t) for d in (2, 1, 3)]
    y_devices = [(f, lax.rem(y + d, ny) * CORES + core) for d in range(1, ny)]
    sibling = (f, y * CORES + 1 - core)
    other_devices = [(device[0], sibling[1]) for device in x_devices]
    right, across, left = (lax.rem(x + d, nx) for d in (1, 2, 3))
    to_right, to_left = x_devices[1], x_devices[2]
    near_devices = [at_z(d) for d in plan.near]
    far_devices = [at_z(d) for d in plan.far]

    loads = [pltpu.make_async_copy(m_hbm, m_ref, load_sem.at[0]), pltpu.make_async_copy(g_hbm, g_ref, load_sem.at[1])]
    for load in loads:
        load.start()
    barrier = pltpu.get_barrier_semaphore()
    peers = far_devices + [at_z(-d) for d in plan.near] + x_devices + y_devices + [sibling] + other_devices
    for device in peers:
        pl.semaphore_signal(barrier, inc=1, device_id=device, device_id_type=MESH)

    basis_own[...] = jnp.zeros_like(basis_own)
    basis_own[0:plan.piece, :] = b_ref[...].astype(BF16)
    chunk = plan.chunk
    for load in loads:
        load.wait()

    def turn(i, carry):
        c = pl.ds(pl.multiple_of(i * chunk, chunk), chunk)
        value = (m_ref[:, c].astype(F32) + g_ref[:, c].astype(F32)).astype(BF16).astype(F32).T
        turned[c, :] = value
        turned_b[c, :] = value.astype(BF16)
        return carry

    lax.fori_loop(0, plan.cols // chunk, turn, 0)
    tiles[...] = jnp.zeros_like(tiles)
    packed[...] = jnp.zeros_like(packed)
    pl.semaphore_wait(barrier, len(peers))

    def begin(src, slots, devices):
        return [comm.start(src, slots.at[i], device) for i, device in enumerate(devices)]

    def add_up(total, slots, copies):
        for i, copy in enumerate(copies):
            copy.wait_recv()
            total = slots[i] if total is None else total + slots[i]
        return total

    def gathered(near):
        return lax.rem(near_id - near + NEAR + NEAR // 2, NEAR)

    slot = basis_in.at[far_id]
    far_copies = [comm.start(basis_own, slot, device) for device in far_devices]
    piece = plan.piece

    def space(i, carry):
        for k in range(FAR):
            n = nx * piece
            lines[...] = turned[pl.ds(pl.multiple_of((i + NEAR * k) * n, 8), n), :]
            for xx in range(nx):
                tiles[xx, k * piece:(k + 1) * piece, :] = lines[xx * piece:(xx + 1) * piece, :]
        for xx in range(nx):
            spread[xx, i] = tiles[xx].T.astype(BF16)
        return carry

    lax.fori_loop(0, NEAR, space, 0)
    for copy in far_copies:
        copy.wait_recv()
    for k in range(FAR):
        packed[k * piece:(k + 1) * piece, :] = basis_in[k, 0:piece].astype(F32)
    basis_buf[x, 0:plan.sent] = packed[...].astype(BF16)

    shifts = [0] + plan.near

    def pass_on(buf, after_batch=None):
        n = plan.sent
        block = buf.at[x, pl.ds(0, n)]
        z_copies = [comm.start(block, buf.at[x, pl.ds((i + 1) * n, n)], near_devices[i])
                    for i in range(NEAR - 1)]
        sent = []
        for a, b in plan.batches:
            for i in range(max(a, 1), b):
                z_copies[i - 1].wait_recv()
            blocks = buf.at[x, pl.ds(a * n, (b - a) * n)]
            sent.append([comm.start(blocks, blocks, device) for device in x_devices])
            if after_batch is not None:
                after_batch(a)
        return sent

    total = jnp.zeros((plan.rows, RANK), F32)
    for (a, b), copies in zip(plan.batches, pass_on(basis_buf)):
        for copy in copies:
            copy.wait_recv()
        for i in range(a, b):
            near = gathered(shifts[i])
            for xx in range(nx):
                total = total + jnp.dot(spread[xx, near][:, :plan.sent],
                                        basis_buf[xx, i * plan.sent:(i + 1) * plan.sent], preferred_element_type=F32)
    part[...] = total

    def half_of(ref, i):
        n = plan.rows // CORES
        return ref.at[pl.ds(pl.multiple_of(i * n, n), n)]

    comm.start(half_of(part, 1 - core), part_c, sibling).wait_recv()
    part_y[y] = half_of(part, core)[...] + part_c[...]
    for copy in [comm.start(part_y.at[y], part_y.at[y], device) for device in y_devices]:
        copy.wait_recv()
    mine = half_of(panel, core)
    total = part_y[0]
    for i in range(1, ny):
        total = total + part_y[i]
    mine[...] = total
    half_copy = comm.start(mine, mine, sibling)

    w = plan.strip

    def strip_rows(i):
        return pl.ds(pl.multiple_of((i * ny + y) * w, w), w)

    half_t[...] = total.T
    for i in range(CORES):
        halves[i] = jnp.dot(half_t[strip_rows(i), :], total, precision=HIGHEST, preferred_element_type=F32)
    copies = [comm.start(halves.at[1 - core], gram_x.at[i], device)
              for i, device in enumerate(other_devices + [sibling])]
    copies += [comm.start(halves.at[core], gram_x.at[i + nx], device) for i, device in enumerate(x_devices)]
    strip[1] = add_up(halves[core], gram_x, copies)
    strip[2] = add_up(strip[1], gram_n, begin(strip.at[1], gram_n, near_devices[::-1]))
    copies = begin(strip.at[2], gram_f, far_devices)
    half_copy.wait_recv()
    gp[:, RANK:] = panel[...].T
    comm.drain(keep=FAR)
    mine = gram_t.at[strip_rows(core)]
    mine[...] = add_up(None, gram_f, copies)
    for copy in [comm.start(mine, mine, device) for device in y_devices]:
        copy.wait_recv()
    mine = half_of(gram_t, core)
    comm.start(mine, mine, sibling).wait_recv()
    gp[:, :RANK] = gram_t[...]

    factor(gp, ot)
    ortho = ot[...].T.astype(BF16)
    ortho_ref[...] = ortho

    rows, group = plan.block, plan.group
    order = plan.near[::-1] + [0]
    pairs = [(o, o + 1) for o in range(0, NEAR, 2)]
    z_copies = []
    sum_n[...] = jnp.zeros_like(sum_n)

    def send_x(pair):
        for o in pair:
            first = lax.rem(near_id + order[o] + NEAR + NEAR // 2, NEAR) * group
            value = jnp.dot(turned_b[pl.ds(pl.multiple_of(first, 16), group), :], ortho, preferred_element_type=F32)
            for xx in range(nx):
                cross[xx, o] = value[xx * rows:(xx + 1) * rows, :]
        a, b = pair
        return [comm.start(cross.at[across, a], cross_r.at[0, a], to_right),
                comm.start(cross.at[across, b], cross_r.at[1, a], to_left)]

    def pass_x(pair, copies):
        a, b = pair
        for copy in copies:
            copy.wait_recv()
        cross[right, a] += cross_r[0, a]
        cross[left, b] += cross_r[1, a]
        return [comm.start(cross.at[xx, pl.ds(a, 2)], cross_x.at[i, pl.ds(a, 2)], device)
                for i, (xx, device) in enumerate(((right, to_right), (left, to_left)))]

    def add_x(pair, copies):
        for copy in copies:
            copy.wait_recv()
        for o in pair:
            total = cross[x, o] + cross_x[0, o] + cross_x[1, o]
            if order[o]:
                sum_x[o] = total
                z_copies.append(comm.start(sum_x.at[o], cross_n.at[o], at_z(order[o])))
            else:
                sum_n[0:rows, :] = add_up(total, cross_n, z_copies)

    first, second = [], []
    for i in range(len(pairs) + 2):
        if i < len(pairs):
            first.append(send_x(pairs[i]))
        if 1 <= i <= len(pairs):
            second.append(pass_x(pairs[i - 1], first[i - 1]))
        if i >= 2:
            add_x(pairs[i - 2], second[i - 2])

    def far_rows(i):
        return pl.ds(pl.multiple_of(i * plan.slot, plan.slot), plan.slot)

    copies = [comm.start(sum_n.at[far_rows(lax.rem(z + d + nz, nz) // NEAR)], cross_f.at[i], device)
              for i, (d, device) in enumerate(zip(plan.far, far_devices))]
    comm.drain(keep=FAR)
    total = add_up(None, cross_f, copies)

    cross_own[...] = total.astype(BF16)
    slot = cross_held.at[far_rows(far_id)]
    far_copies = [comm.start(cross_own, slot, device) for device in far_devices]
    sq[0] = jnp.broadcast_to(jnp.sum(total * total, axis=0, keepdims=True), (8, RANK))
    sq_copies = begin(sq.at[0], sq_f, far_devices)
    comm.drain(keep=2 * FAR)
    for copy in far_copies:
        copy.wait_recv()
    cross_buf[x, 0:plan.sent] = cross_held[0:plan.sent, :]

    def after_batch(a):
        if a == 0:
            sq[1] = add_up(None, sq_f, sq_copies)
            later.append(begin(sq.at[1], sq_n, near_devices))
        if a == 1:
            sq[2] = add_up(sq[1], sq_n, later[0])
            later.append(begin(sq.at[2], sq_x, x_devices))

    later = []
    batches = list(zip(plan.batches, pass_on(cross_buf, after_batch)))
    sq[3] = add_up(sq[2], sq_x, later[1])
    sq_copies = begin(sq.at[3], sq_y, y_devices)

    def settle(batch):
        (a, b), copies = batch
        for copy in copies:
            copy.wait_recv()
        for i in range(a, b):
            for xx in range(nx):
                nat[xx * rows:(xx + 1) * rows, :] = cross_buf[xx, i * plan.sent:i * plan.sent + rows].astype(F32)
            first = pl.multiple_of(gathered(shifts[i]) * group, 16)
            piece_ref[pl.ds(first, group), :] = nat[...].astype(BF16)

    for batch in batches[:-1]:
        settle(batch)
    sq[4] = add_up(sq[3], sq_y, sq_copies)
    last = comm.start(sq.at[4], sq_c.at[0], sibling)
    settle(batches[-1])
    scale_ref[...] = 1.0 / jnp.sqrt(add_up(sq[4], sq_c, [last])[0:1, :] + 1e-06)
    comm.drain()


def exchange(plan, momentum, gradient, basis):
    nx, ny, near, far = plan.nx, plan.ny, len(plan.near), len(plan.far)
    w, half = plan.strip, plan.rows // CORES

    def f32(*shape):
        return pltpu.VMEM((*shape, RANK), F32)

    def bf16(*shape):
        return pltpu.VMEM((*shape, RANK), BF16)

    whole = pltpu.VMEM((plan.rows, plan.cols), BF16)
    scratch = [
        whole, whole, f32(plan.cols), bf16(plan.cols), f32(nx * plan.piece), f32(nx, FAR * plan.slot),
        pltpu.VMEM((nx, NEAR, plan.rows, FAR * plan.slot), BF16), bf16(plan.slot), bf16(FAR, plan.slot),
        f32(plan.sent), bf16(nx, NEAR * plan.sent),
        f32(plan.rows), f32(half), f32(ny, half), f32(plan.rows),
        pltpu.VMEM((RANK, half), F32), f32(CORES, w), f32(3, w), f32(2 * nx - 1, w), f32(near, w), f32(far, w), f32(RANK),
        pltpu.VMEM((RANK, RANK + plan.rows), F32), pltpu.VMEM((RANK, plan.rows), F32),
        f32(nx, NEAR, plan.block), f32(2, NEAR, plan.block), f32(2, NEAR, plan.block), f32(near, plan.block), f32(near, plan.block),
        f32(FAR * plan.slot), f32(far, plan.slot), bf16(plan.slot), bf16(FAR * plan.slot), bf16(nx, NEAR * plan.sent),
        f32(plan.group),
        f32(5, 8), f32(far, 8), f32(near, 8), f32(nx - 1, 8), f32(max(ny - 1, 1), 8), f32(1, 8),
        pltpu.SemaphoreType.DMA((n_copies(plan),)),
        pltpu.SemaphoreType.DMA((n_copies(plan),)),
        pltpu.SemaphoreType.DMA((2,)),
    ]
    vmem, hbm = pl.BlockSpec(memory_space=pltpu.VMEM), pl.BlockSpec(memory_space=pl.ANY)
    return pl.pallas_call(
        functools.partial(kernel, plan),
        out_shape=(
            jax.ShapeDtypeStruct((plan.rows, RANK), BF16),
            jax.ShapeDtypeStruct((plan.cols, RANK), BF16),
            jax.ShapeDtypeStruct((1, RANK), F32),
        ),
        in_specs=[hbm, hbm, vmem],
        out_specs=(vmem,) * 3,
        scratch_shapes=scratch,
        compiler_params=pltpu.CompilerParams(
            collective_id=0, has_side_effects=True, vmem_limit_bytes=56 * 1024 * 1024),
        cost_estimate=pl.CostEstimate(
            flops=4 * plan.rows * plan.cols * RANK, bytes_accessed=6 * plan.rows * plan.cols, transcendentals=0),
        name="dion_exchange",
    )(momentum, gradient, basis)


def write(scale, m_ref, g_ref, ortho_ref, piece_ref, scale_ref, update_ref, moved_ref):
    ortho, scaleinv = ortho_ref[...], scale_ref[...]
    n = 128 if piece_ref.shape[0] % 128 == 0 else piece_ref.shape[0]
    dims = (((1,), (1,)), ((), ()))
    for i in range(0, piece_ref.shape[0], n):
        c = slice(i, i + n)
        piece = piece_ref[c, :]
        newbasis = (piece.astype(F32) * scaleinv).astype(BF16)
        update = scale * lax.dot_general(ortho, newbasis, dims, preferred_element_type=F32)
        update_ref[:, c] = update.astype(BF16)
        summed = m_ref[:, c].astype(F32) + g_ref[:, c].astype(F32)
        moved = summed - 0.05 * lax.dot_general(ortho, piece, dims, preferred_element_type=F32)
        moved_ref[:, c] = moved.astype(BF16)


def outputs(scale, momentum, gradient, ortho, piece, scaleinv):
    rows, cols = momentum.shape
    steps = 2 if cols % 256 == 0 else 1
    wide = pl.BlockSpec((rows, cols // steps), lambda i: (0, i))
    return pl.pallas_call(
        functools.partial(write, scale),
        out_shape=(jax.ShapeDtypeStruct((rows, cols), BF16),) * 2,
        grid=(steps,),
        in_specs=[
            wide, wide, pl.BlockSpec((rows, RANK), lambda i: (0, 0)),
            pl.BlockSpec((cols // steps, RANK), lambda i: (i, 0)), pl.BlockSpec((1, RANK), lambda i: (0, 0)),
        ],
        out_specs=(wide, wide),
        compiler_params=pltpu.CompilerParams(vmem_limit_bytes=32 * 1024 * 1024),
        cost_estimate=pl.CostEstimate(
            flops=4 * rows * cols * RANK, bytes_accessed=8 * rows * cols + 2 * cols * RANK, transcendentals=0),
        name="dion_outputs",
    )(momentum, gradient, ortho, piece, scaleinv)


def solution(mesh):
    n_fsdp, n_tensor = mesh.shape["fsdp"], mesh.shape["tensor"]

    def body(momentum, gradient, basis):
        rows, cols = momentum.shape
        plan = Plan(n_fsdp, n_tensor, rows, cols)
        scale = math.sqrt(rows * n_fsdp * cols * n_tensor / RANK)
        ortho, piece, scaleinv = exchange(plan, momentum, gradient, basis)
        return outputs(scale, momentum, gradient, ortho, piece, scaleinv)

    in_specs = (P("fsdp", "tensor"), P("fsdp", "tensor"), P(("tensor", "fsdp"), None))
    out_specs = (P("fsdp", "tensor"), P("fsdp", "tensor"))
    return jax.shard_map(body, mesh=mesh, in_specs=in_specs, out_specs=out_specs, check_vma=False)
```

```python
import functools
import math

import jax
import jax.numpy as jnp
from jax import lax
from jax.experimental import pallas as pl
from jax.experimental.pallas import tpu as pltpu
from jax.sharding import PartitionSpec as P

MESH = pl.DeviceIdType.MESH
HIGHEST = lax.Precision.HIGHEST
RANK = 128
NX = 4
NEAR = 8
FAR = 4
CORES = 2
F32 = jnp.float32
BF16 = jnp.bfloat16


class Plan:
    def __init__(self, n_fsdp, n_tensor, rows, cols):
        self.nz, self.nx, self.nt, self.ny = n_fsdp // NX, NX, n_tensor, n_tensor // CORES
        assert self.nz == NEAR * FAR and NX == 4
        self.rows, self.cols = rows, cols
        self.piece = cols // n_fsdp
        self.slot = -(-self.piece // 16) * 16
        self.block = self.piece * FAR
        self.sent = -(-self.block // 16) * 16
        self.group = self.block * NX
        self.near = sorted([d for d in range(-((NEAR - 1) // 2), NEAR // 2 + 1) if d], key=abs)
        self.far = [(2 * i + 1) * (NEAR // 2) for i in range(-(FAR // 2), FAR // 2)]
        self.far.sort(key=abs, reverse=True)
        self.strip = RANK // n_tensor
        self.chunk = 256 if cols % 256 == 0 else cols // self.nx
        edges = [0] + [e for e in (1, 3, 5) if e < NEAR] + [NEAR]
        self.batches = list(zip(edges, edges[1:]))


class Copies:
    def __init__(self, send, recv):
        self.send, self.recv, self.used, self.out = send, recv, 0, []

    def start(self, src, dst, device):
        i = self.used
        self.used += 1
        copy = pltpu.make_async_remote_copy(
            src_ref=src, dst_ref=dst, send_sem=self.send.at[i], recv_sem=self.recv.at[i],
            device_id=device, device_id_type=MESH,
        )
        copy.start()
        self.out.append(copy)
        return copy

    def drain(self, keep=0):
        n = len(self.out) - keep
        for copy in self.out[:n]:
            copy.wait_send()
        self.out = self.out[n:]


def n_copies(plan):
    near, far, x, y = len(plan.near), len(plan.far), plan.nx - 1, plan.ny - 1
    gather = far + near + x * len(plan.batches)
    return 2 * gather + (y + 2) + (2 * x + 1 + near + far + y + 1) + (2 * NEAR + near + far) + (far + near + x + y + 1)


def factor(gp_ref, ot_ref):
    n, nb = RANK, 32
    lane1 = lax.broadcasted_iota(jnp.int32, (1, n), 1)
    for top in range(0, n, nb):
        lane = lax.broadcasted_iota(jnp.int32, (n - top, n), 1)
        row1 = lax.broadcasted_iota(jnp.int32, (n - top, 1), 0) + top

        def step(s, carry, top=top, lane=lane, row1=row1):
            j = top + s * 4
            gram = gp_ref[top:, :n]
            cols, rows = [], []
            for p in range(4):
                rows.append(gp_ref[pl.ds(j + p, 1), :])
                cols.append(jnp.sum(jnp.where(lane == j + p, gram, 0.0), axis=1, keepdims=True))
            a = [[jnp.sum(jnp.where(lane1 == j + q, rows[p][:, :n], 0.0), axis=1, keepdims=True)
                  for q in range(p + 1)] for p in range(4)]
            inv, mults = [], []
            for p in range(4):
                for q in range(p):
                    low = a[p][q] * inv[q]
                    rows[p] = rows[p] - low * rows[q]
                    cols[p] = cols[p] - low * cols[q]
                    for r in range(p, 4):
                        a[r][p] = a[r][p] - low * a[r][q]
                inv.append(1.0 / a[p][p])
                mults.append(jnp.where(row1 > j + 3, cols[p] * inv[p], 0.0))
                ot_ref[pl.ds(j + p, 1), :] = rows[p][:, n:] * (1.0 / jnp.sqrt(a[p][p]))
            new = gp_ref[top:, :]
            for p in range(4):
                new = new - mults[p] * rows[p]
            gp_ref[top:, :] = new
            return carry

        lax.fori_loop(0, nb // 4, step, 0)


def kernel(plan, m_hbm, g_hbm, b_ref, ortho_ref, piece_ref, scale_ref,
           m_ref, g_ref, turned, turned_b, lines, tiles, spread, basis_own, basis_in, packed, basis_buf,
           part, part_c, part_y, panel, half_t, halves, strip, gram_x, gram_n, gram_f, gram_t, gp, ot,
           cross, cross_r, cross_x, sum_x, cross_n, sum_n, cross_f, cross_own, cross_held, cross_buf, nat,
           sq, sq_f, sq_n, sq_x, sq_y, sq_c, send_sem, recv_sem, load_sem):
    f, t = lax.axis_index("fsdp"), lax.axis_index("tensor")
    nz, nx, ny = plan.nz, plan.nx, plan.ny
    z, x = f // nx, f % nx
    y, core = t // CORES, t % CORES
    near_id, far_id = z % NEAR, z // NEAR
    comm = Copies(send_sem, recv_sem)

    def at_z(d):
        return (lax.rem(z + d + nz, nz) * nx + x, t)

    x_devices = [(z * nx + lax.rem(x + d, nx), t) for d in (2, 1, 3)]
    y_devices = [(f, lax.rem(y + d, ny) * CORES + core) for d in range(1, ny)]
    sibling = (f, y * CORES + 1 - core)
    other_devices = [(device[0], sibling[1]) for device in x_devices]
    right, across, left = (lax.rem(x + d, nx) for d in (1, 2, 3))
    to_right, to_left = x_devices[1], x_devices[2]
    near_devices = [at_z(d) for d in plan.near]
    far_devices = [at_z(d) for d in plan.far]

    loads = [pltpu.make_async_copy(m_hbm, m_ref, load_sem.at[0]), pltpu.make_async_copy(g_hbm, g_ref, load_sem.at[1])]
    for load in loads:
        load.start()
    barrier = pltpu.get_barrier_semaphore()
    peers = far_devices + [at_z(-d) for d in plan.near] + x_devices + y_devices + [sibling] + other_devices
    for device in peers:
        pl.semaphore_signal(barrier, inc=1, device_id=device, device_id_type=MESH)

    basis_own[...] = jnp.zeros_like(basis_own)
    basis_own[0:plan.piece, :] = b_ref[...].astype(BF16)
    chunk = plan.chunk
    for load in loads:
        load.wait()

    def turn(i, carry):
        c = pl.ds(pl.multiple_of(i * chunk, chunk), chunk)
        value = (m_ref[:, c].astype(F32) + g_ref[:, c].astype(F32)).astype(BF16).astype(F32).T
        turned[c, :] = value
        turned_b[c, :] = value.astype(BF16)
        return carry

    lax.fori_loop(0, plan.cols // chunk, turn, 0)
    tiles[...] = jnp.zeros_like(tiles)
    packed[...] = jnp.zeros_like(packed)
    pl.semaphore_wait(barrier, len(peers))

    def begin(src, slots, devices):
        return [comm.start(src, slots.at[i], device) for i, device in enumerate(devices)]

    def add_up(total, slots, copies):
        for i, copy in enumerate(copies):
            copy.wait_recv()
            total = slots[i] if total is None else total + slots[i]
        return total

    def gathered(near):
        return lax.rem(near_id - near + NEAR + NEAR // 2, NEAR)

    slot = basis_in.at[far_id]
    far_copies = [comm.start(basis_own, slot, device) for device in far_devices]
    piece = plan.piece

    def space(i, carry):
        for k in range(FAR):
            n = nx * piece
            lines[...] = turned[pl.ds(pl.multiple_of((i + NEAR * k) * n, 8), n), :]
            for xx in range(nx):
                tiles[xx, k * piece:(k + 1) * piece, :] = lines[xx * piece:(xx + 1) * piece, :]
        for xx in range(nx):
            spread[xx, i] = tiles[xx].T.astype(BF16)
        return carry

    lax.fori_loop(0, NEAR, space, 0)
    for copy in far_copies:
        copy.wait_recv()
    for k in range(FAR):
        packed[k * piece:(k + 1) * piece, :] = basis_in[k, 0:piece].astype(F32)
    basis_buf[x, 0:plan.sent] = packed[...].astype(BF16)

    shifts = [0] + plan.near

    def pass_on(buf, after_batch=None):
        n = plan.sent
        block = buf.at[x, pl.ds(0, n)]
        z_copies = [comm.start(block, buf.at[x, pl.ds((i + 1) * n, n)], near_devices[i])
                    for i in range(NEAR - 1)]
        sent = []
        for a, b in plan.batches:
            for i in range(max(a, 1), b):
                z_copies[i - 1].wait_recv()
            blocks = buf.at[x, pl.ds(a * n, (b - a) * n)]
            sent.append([comm.start(blocks, blocks, device) for device in x_devices])
            if after_batch is not None:
                after_batch(a)
        return sent

    total = jnp.zeros((plan.rows, RANK), F32)
    for (a, b), copies in zip(plan.batches, pass_on(basis_buf)):
        for copy in copies:
            copy.wait_recv()
        for i in range(a, b):
            near = gathered(shifts[i])
            for xx in range(nx):
                total = total + jnp.dot(spread[xx, near][:, :plan.sent],
                                        basis_buf[xx, i * plan.sent:(i + 1) * plan.sent], preferred_element_type=F32)
    part[...] = total

    def half_of(ref, i):
        n = plan.rows // CORES
        return ref.at[pl.ds(pl.multiple_of(i * n, n), n)]

    comm.start(half_of(part, 1 - core), part_c, sibling).wait_recv()
    part_y[y] = half_of(part, core)[...] + part_c[...]
    for copy in [comm.start(part_y.at[y], part_y.at[y], device) for device in y_devices]:
        copy.wait_recv()
    mine = half_of(panel, core)
    total = part_y[0]
    for i in range(1, ny):
        total = total + part_y[i]
    mine[...] = total
    half_copy = comm.start(mine, mine, sibling)

    w = plan.strip

    def strip_rows(i):
        return pl.ds(pl.multiple_of((i * ny + y) * w, w), w)

    half_t[...] = total.T
    for i in range(CORES):
        halves[i] = jnp.dot(half_t[strip_rows(i), :], total, precision=HIGHEST, preferred_element_type=F32)
    copies = [comm.start(halves.at[1 - core], gram_x.at[i], device)
              for i, device in enumerate(other_devices + [sibling])]
    copies += [comm.start(halves.at[core], gram_x.at[i + nx], device) for i, device in enumerate(x_devices)]
    strip[1] = add_up(halves[core], gram_x, copies)
    strip[2] = add_up(strip[1], gram_n, begin(strip.at[1], gram_n, near_devices[::-1]))
    copies = begin(strip.at[2], gram_f, far_devices)
    half_copy.wait_recv()
    gp[:, RANK:] = panel[...].T
    comm.drain(keep=FAR)
    mine = gram_t.at[strip_rows(core)]
    mine[...] = add_up(None, gram_f, copies)
    for copy in [comm.start(mine, mine, device) for device in y_devices]:
        copy.wait_recv()
    mine = half_of(gram_t, core)
    comm.start(mine, mine, sibling).wait_recv()
    gp[:, :RANK] = gram_t[...]

    factor(gp, ot)
    ortho = ot[...].T.astype(BF16)
    ortho_ref[...] = ortho

    rows, group = plan.block, plan.group
    order = plan.near[::-1] + [0]
    pairs = [(o, o + 1) for o in range(0, NEAR, 2)]
    z_copies = []
    sum_n[...] = jnp.zeros_like(sum_n)

    def send_x(pair):
        for o in pair:
            first = lax.rem(near_id + order[o] + NEAR + NEAR // 2, NEAR) * group
            value = jnp.dot(turned_b[pl.ds(pl.multiple_of(first, 16), group), :], ortho, preferred_element_type=F32)
            for xx in range(nx):
                cross[xx, o] = value[xx * rows:(xx + 1) * rows, :]
        a, b = pair
        return [comm.start(cross.at[across, a], cross_r.at[0, a], to_right),
                comm.start(cross.at[across, b], cross_r.at[1, a], to_left)]

    def pass_x(pair, copies):
        a, b = pair
        for copy in copies:
            copy.wait_recv()
        cross[right, a] += cross_r[0, a]
        cross[left, b] += cross_r[1, a]
        return [comm.start(cross.at[xx, pl.ds(a, 2)], cross_x.at[i, pl.ds(a, 2)], device)
                for i, (xx, device) in enumerate(((right, to_right), (left, to_left)))]

    def add_x(pair, copies):
        for copy in copies:
            copy.wait_recv()
        for o in pair:
            total = cross[x, o] + cross_x[0, o] + cross_x[1, o]
            if order[o]:
                sum_x[o] = total
                z_copies.append(comm.start(sum_x.at[o], cross_n.at[o], at_z(order[o])))
            else:
                sum_n[0:rows, :] = add_up(total, cross_n, z_copies)

    first, second = [], []
    for i in range(len(pairs) + 2):
        if i < len(pairs):
            first.append(send_x(pairs[i]))
        if 1 <= i <= len(pairs):
            second.append(pass_x(pairs[i - 1], first[i - 1]))
        if i >= 2:
            add_x(pairs[i - 2], second[i - 2])

    def far_rows(i):
        return pl.ds(pl.multiple_of(i * plan.slot, plan.slot), plan.slot)

    copies = [comm.start(sum_n.at[far_rows(lax.rem(z + d + nz, nz) // NEAR)], cross_f.at[i], device)
              for i, (d, device) in enumerate(zip(plan.far, far_devices))]
    comm.drain(keep=FAR)
    total = add_up(None, cross_f, copies)

    cross_own[...] = total.astype(BF16)
    slot = cross_held.at[far_rows(far_id)]
    far_copies = [comm.start(cross_own, slot, device) for device in far_devices]
    sq[0] = jnp.broadcast_to(jnp.sum(total * total, axis=0, keepdims=True), (8, RANK))
    sq_copies = begin(sq.at[0], sq_f, far_devices)
    comm.drain(keep=2 * FAR)
    for copy in far_copies:
        copy.wait_recv()
    cross_buf[x, 0:plan.sent] = cross_held[0:plan.sent, :]

    def after_batch(a):
        if a == 0:
            sq[1] = add_up(None, sq_f, sq_copies)
            later.append(begin(sq.at[1], sq_n, near_devices))
        if a == 1:
            sq[2] = add_up(sq[1], sq_n, later[0])
            later.append(begin(sq.at[2], sq_x, x_devices))

    later = []
    batches = list(zip(plan.batches, pass_on(cross_buf, after_batch)))
    sq[3] = add_up(sq[2], sq_x, later[1])
    sq_copies = begin(sq.at[3], sq_y, y_devices)

    def settle(batch):
        (a, b), copies = batch
        for copy in copies:
            copy.wait_recv()
        for i in range(a, b):
            for xx in range(nx):
                nat[xx * rows:(xx + 1) * rows, :] = cross_buf[xx, i * plan.sent:i * plan.sent + rows].astype(F32)
            first = pl.multiple_of(gathered(shifts[i]) * group, 16)
            piece_ref[pl.ds(first, group), :] = nat[...].astype(BF16)

    for batch in batches[:-1]:
        settle(batch)
    sq[4] = add_up(sq[3], sq_y, sq_copies)
    last = comm.start(sq.at[4], sq_c.at[0], sibling)
    settle(batches[-1])
    scale_ref[...] = 1.0 / jnp.sqrt(add_up(sq[4], sq_c, [last])[0:1, :] + 1e-06)
    comm.drain()


def exchange(plan, momentum, gradient, basis):
    nx, ny, near, far = plan.nx, plan.ny, len(plan.near), len(plan.far)
    w, half = plan.strip, plan.rows // CORES

    def f32(*shape):
        return pltpu.VMEM((*shape, RANK), F32)

    def bf16(*shape):
        return pltpu.VMEM((*shape, RANK), BF16)

    whole = pltpu.VMEM((plan.rows, plan.cols), BF16)
    scratch = [
        whole, whole, f32(plan.cols), bf16(plan.cols), f32(nx * plan.piece), f32(nx, FAR * plan.slot),
        pltpu.VMEM((nx, NEAR, plan.rows, FAR * plan.slot), BF16), bf16(plan.slot), bf16(FAR, plan.slot),
        f32(plan.sent), bf16(nx, NEAR * plan.sent),
        f32(plan.rows), f32(half), f32(ny, half), f32(plan.rows),
        pltpu.VMEM((RANK, half), F32), f32(CORES, w), f32(3, w), f32(2 * nx - 1, w), f32(near, w), f32(far, w), f32(RANK),
        pltpu.VMEM((RANK, RANK + plan.rows), F32), pltpu.VMEM((RANK, plan.rows), F32),
        f32(nx, NEAR, plan.block), f32(2, NEAR, plan.block), f32(2, NEAR, plan.block), f32(near, plan.block), f32(near, plan.block),
        f32(FAR * plan.slot), f32(far, plan.slot), bf16(plan.slot), bf16(FAR * plan.slot), bf16(nx, NEAR * plan.sent),
        f32(plan.group),
        f32(5, 8), f32(far, 8), f32(near, 8), f32(nx - 1, 8), f32(max(ny - 1, 1), 8), f32(1, 8),
        pltpu.SemaphoreType.DMA((n_copies(plan),)),
        pltpu.SemaphoreType.DMA((n_copies(plan),)),
        pltpu.SemaphoreType.DMA((2,)),
    ]
    vmem, hbm = pl.BlockSpec(memory_space=pltpu.VMEM), pl.BlockSpec(memory_space=pl.ANY)
    return pl.pallas_call(
        functools.partial(kernel, plan),
        out_shape=(
            jax.ShapeDtypeStruct((plan.rows, RANK), BF16),
            jax.ShapeDtypeStruct((plan.cols, RANK), BF16),
            jax.ShapeDtypeStruct((1, RANK), F32),
        ),
        in_specs=[hbm, hbm, vmem],
        out_specs=(vmem,) * 3,
        scratch_shapes=scratch,
        compiler_params=pltpu.CompilerParams(
            collective_id=0, has_side_effects=True, vmem_limit_bytes=56 * 1024 * 1024),
        cost_estimate=pl.CostEstimate(
            flops=4 * plan.rows * plan.cols * RANK, bytes_accessed=6 * plan.rows * plan.cols, transcendentals=0),
        name="dion_exchange",
    )(momentum, gradient, basis)


def write(scale, m_ref, g_ref, ortho_ref, piece_ref, scale_ref, update_ref, moved_ref):
    ortho, scaleinv = ortho_ref[...], scale_ref[...]
    n = 128 if piece_ref.shape[0] % 128 == 0 else piece_ref.shape[0]
    dims = (((1,), (1,)), ((), ()))
    for i in range(0, piece_ref.shape[0], n):
        c = slice(i, i + n)
        piece = piece_ref[c, :]
        newbasis = (piece.astype(F32) * scaleinv).astype(BF16)
        update = scale * lax.dot_general(ortho, newbasis, dims, preferred_element_type=F32)
        update_ref[:, c] = update.astype(BF16)
        summed = m_ref[:, c].astype(F32) + g_ref[:, c].astype(F32)
        moved = summed - 0.05 * lax.dot_general(ortho, piece, dims, preferred_element_type=F32)
        moved_ref[:, c] = moved.astype(BF16)


def outputs(scale, momentum, gradient, ortho, piece, scaleinv):
    rows, cols = momentum.shape
    steps = 2 if cols % 256 == 0 else 1
    wide = pl.BlockSpec((rows, cols // steps), lambda i: (0, i))
    return pl.pallas_call(
        functools.partial(write, scale),
        out_shape=(jax.ShapeDtypeStruct((rows, cols), BF16),) * 2,
        grid=(steps,),
        in_specs=[
            wide, wide, pl.BlockSpec((rows, RANK), lambda i: (0, 0)),
            pl.BlockSpec((cols // steps, RANK), lambda i: (i, 0)), pl.BlockSpec((1, RANK), lambda i: (0, 0)),
        ],
        out_specs=(wide, wide),
        compiler_params=pltpu.CompilerParams(vmem_limit_bytes=63 * 1024 * 1024),
        cost_estimate=pl.CostEstimate(
            flops=4 * rows * cols * RANK, bytes_accessed=8 * rows * cols + 2 * cols * RANK, transcendentals=0),
        name="dion_outputs",
    )(momentum, gradient, ortho, piece, scaleinv)


def solution(mesh):
    n_fsdp, n_tensor = mesh.shape["fsdp"], mesh.shape["tensor"]

    def body(momentum, gradient, basis):
        rows, cols = momentum.shape
        plan = Plan(n_fsdp, n_tensor, rows, cols)
        scale = math.sqrt(rows * n_fsdp * cols * n_tensor / RANK)
        ortho, piece, scaleinv = exchange(plan, momentum, gradient, basis)
        return outputs(scale, momentum, gradient, ortho, piece, scaleinv)

    in_specs = (P("fsdp", "tensor"), P("fsdp", "tensor"), P(("tensor", "fsdp"), None))
    out_specs = (P("fsdp", "tensor"), P("fsdp", "tensor"))
    return jax.shard_map(body, mesh=mesh, in_specs=in_specs, out_specs=out_specs, check_vma=False)
```
